1024 devices in a mesh: rep: 8 (over z_lo), node: 8 (over z_hi, core), shard: 16 (over x, y).
Axes of the slice: x: 4, y: 4, z: 32 (z_hi: 4, z_lo: 8; z = z_hi * 8 + z_lo), core: 2. Of those that a mesh axis runs over, the one named last changes fastest.
Arguments:
- hidden_in: bfloat16 [131072, 768], P(('rep', 'node', 'shard')), may hold values from -6 to 6
- expert_ids: int32 [131072, 1], P(('rep', 'node', 'shard')), may hold values from 0 to 7; in each aligned block of 128 rows (0 to 127, 128 to 255, ...) at most 24 rows name the same one
- gate_prob: float32 [131072], P(('rep', 'node', 'shard')), may hold values from 0.1 to 1
- out_grad: bfloat16 [131072, 2048], P(('rep', 'node', 'shard')), may hold values from -24 to 24
- codes: bfloat16 [8, 768, 2048], P('node', None, 'shard'), may hold values from -4 to 4
- scales: float32 [8, 768], P('node'), may hold values from 0.010825317 to 0.10825317
Outputs:
- mixed: bfloat16 [131072, 2048], P(('rep', 'node', 'shard'))
- hidden_grad: bfloat16 [131072, 768], P(('rep', 'node', 'shard'))
- code_grad: float32 [8, 768, 2048], P('node', 'rep', 'shard')
The draws below stay inside these ranges and needn't reach their ends.
Inputs may be any that keep to these rules, and one draw needn't show every extreme that they name: `expert_ids`: no expert is chosen by more than 24 tokens of one device; that many is reached on some device.
All inputs are finite; a program needn't handle non-finite values.
Results may differ from the reference program's by a relative error of at most 0.022.
Values may be sent and summed in bfloat16 or wider, within the bound.
A program may use at most 32 MiB of HBM per device.

```python
import math
import jax
import jax.numpy as jnp
import numpy as np
from jax import lax

D_WIN = 2048
F_WIN = 768
TOK_DEV = 128
EXPERTS = 8
CAP = 24
TOKENS = 131072
N_REP = 8
N_NODE = 8
N_SHARD = 16


def with_spikes(result, rng, source, target, blocks, factor):
    def block_of(axis_at):
        return (jnp.arange(result.shape[axis_at]) // (result.shape[axis_at] // blocks)).reshape((-1,) + (1,) * (result.ndim - 1 - axis_at))

    one_side = jax.random.permutation(rng, blocks)[block_of(target)]
    far = (block_of(target) + blocks // 2) % blocks
    return jnp.where((block_of(source) == one_side) | (block_of(source) == far), factor * result, result)


def levels(stream_key, extent, split, least, top_value):
    level, own = 1.0, jax.random.fold_in(stream_key, 6)
    for dim, parts in split:
        steps = jnp.exp(jax.random.uniform(jax.random.fold_in(own, dim), (parts,), jnp.float32, least / len(split), top_value / len(split)))
        level = level * jnp.repeat(steps, extent[dim] // parts).reshape([-1 if axis == dim else 1 for axis in range(len(extent))])
    return level


def shared_out(own_key, own, number, rows, amount, top, bound, slope):
    sequence = jax.random.permutation(own_key, amount)
    packed, ordinary = portions_of(amount, rows * top, bound, slope, True), portions_of(amount, rows * top, bound, slope, False)
    places = jnp.arange(amount)

    def named(tallies, offset_by):
        used = int((tallies > 0).sum())
        fixed = max(1, used // 4)
        moved = fixed + (places - fixed + offset_by * (used - fixed)) % max(1, amount - fixed)
        return jnp.zeros((amount,), jnp.int32).at[sequence[jnp.where(places < fixed, places, moved)]].set(jnp.asarray(tallies, jnp.int32))

    tallies = jnp.where(number % 4 == 0, named(packed, number // 4), named(ordinary, number - number // 4 - 1))
    mixed = jax.random.permutation(jax.random.fold_in(own, 3), amount)
    giver, sink = mixed[0:amount // 2 * 2:2], mixed[1:amount // 2 * 2:2]
    margin = jnp.minimum(tallies[giver] - 1, bound - tallies[sink]) // 2
    margin = jnp.where((giver == sequence[0]) | (sink == sequence[0]) | (tallies[sink] == 0), 0, jnp.maximum(margin, 0))
    moved = jax.random.randint(jax.random.fold_in(own, 4), (amount // 2,), 0, 1 << 20) % (margin + 1)
    tallies = tallies.at[giver].add(-moved).at[sink].add(moved)
    items = jnp.searchsorted(jnp.cumsum(tallies), jnp.arange(rows * top), side="right").astype(jnp.int32)
    listing = items.reshape(top, rows).T
    listing = listing[jax.random.permutation(jax.random.fold_in(own, 1), rows)]
    offset_by = jax.random.randint(jax.random.fold_in(own, 2), (rows, 1), 0, top)
    return jnp.take_along_axis(listing, (jnp.arange(top)[None, :] + offset_by) % top, axis=1)


def portions_of(count, total, bound, slope, full):
    weights = [(1 << 20) // math.isqrt(standing ** slope) + 1 for standing in range(1, count + 1)]
    largest = bound if full else min(bound, max(-(-total // count), total * weights[0] // sum(weights)))
    least = 1 if total - largest >= count - 1 else 0
    holding, rest = [largest] + [least] * (count - 1), total - largest - least * (count - 1)
    while rest > 0:
        movable = [i for i in range(1, count) if holding[i] < largest] or [i for i in range(1, count) if holding[i] < bound]
        mass, left = sum([weights[i] for i in movable]), rest
        for i in movable:
            addition = min(bound - holding[i], max(1, left * weights[i] // mass), rest)
            holding[i] = holding[i] + addition
            rest = rest - addition
    return np.array(holding)


def noise(key, shape, deviation, reach, split=(), held_as=jnp.bfloat16):
    entries = deviation * jax.random.normal(key, shape, jnp.float32)
    if split:
        entries = entries * levels(key, shape, split, -0.22, 0.18)
    return jnp.clip(entries, -reach, reach).astype(held_as)


def gaussian_with(rng, shape, deviation, bound, cuts, heavy, kind=jnp.bfloat16):
    drawn = deviation * jax.random.normal(rng, shape, jnp.float32)
    if cuts:
        drawn = drawn * levels(rng, shape, cuts, -0.22, 0.18)
    return jnp.clip(with_spikes(drawn, jax.random.fold_in(rng, 3), *heavy), -bound, bound).astype(kind)


def setup_inputs(seed: int = 0) -> dict:
    seeds = jax.random.split(jax.random.key(seed), 7)
    hidden_in = noise(seeds[0], (TOKENS, F_WIN), 1.0, 6.0, ((0, 1024),))
    expert_ids_keys = jax.random.split(jax.random.fold_in(seeds[1], 1), TOKENS // TOK_DEV)
    expert_ids_turns = jax.random.permutation(jax.random.fold_in(seeds[1], 3), TOKENS // TOK_DEV)
    expert_ids = jax.vmap(lambda own, number: shared_out(jax.random.fold_in(seeds[1], 2), own, number, TOK_DEV, EXPERTS, 1, CAP, 2))(expert_ids_keys, expert_ids_turns).reshape((TOKENS, 1))
    gate_prob = jnp.clip(jnp.exp(math.log(1.0) - 2.3025851 * jax.random.uniform(seeds[2], (TOKENS,), jnp.float32) ** levels(seeds[2], (TOKENS,), ((0, 1024),), -0.2, 0.2)), 0.1, 1.0)
    out_grad = gaussian_with(seeds[3], (TOKENS, D_WIN), 1.0, 24.0, ((0, 1024),), (0, 1, 1024, 6.0))
    codes = noise(seeds[4], (EXPERTS, F_WIN, D_WIN), 1.0, 4.0, ((0, 8), (2, 16)))
    scales = jnp.clip(jnp.exp(math.log(0.10825317) - 2.3025851 * jax.random.uniform(seeds[5], (EXPERTS, F_WIN), jnp.float32) ** levels(seeds[5], (EXPERTS, F_WIN), ((0, 8),), -0.2, 0.2)), 0.010825317, 0.10825317)
    return {"hidden_in": hidden_in, "expert_ids": expert_ids, "gate_prob": gate_prob, "out_grad": out_grad, "codes": codes, "scales": scales}


def regroup(values):
    shaped = values.reshape((N_REP, N_NODE, N_SHARD, TOK_DEV) + values.shape[1:])
    shaped = jnp.swapaxes(shaped, 1, 2)
    return shaped.reshape((N_REP * N_SHARD, N_NODE * TOK_DEV) + values.shape[1:])


def ungroup(values):
    shaped = values.reshape((N_REP, N_SHARD, N_NODE, TOK_DEV) + values.shape[2:])
    shaped = jnp.swapaxes(shaped, 1, 2)
    return shaped.reshape((TOKENS,) + values.shape[2:])


def reference(hidden_in, expert_ids, gate_prob, out_grad, codes, scales):
    experts = codes.shape[0]
    weight = (codes.astype(jnp.float32) * scales[:, :, None]).astype(jnp.bfloat16)
    weight = lax.optimization_barrier(weight).astype(jnp.float32)
    scaled = (gate_prob[:, None] * out_grad.astype(jnp.float32)).astype(jnp.bfloat16)
    group_cap = N_NODE * CAP
    hidden_groups = regroup(hidden_in)
    scaled_groups = regroup(scaled)
    id_groups = regroup(expert_ids[:, 0])

    def one_group(total, pieces):
        hidden_rows, scaled_rows, id_rows = pieces
        onehot = (id_rows[:, None] == jnp.arange(experts, dtype=jnp.int32)[None, :]).astype(jnp.int32)
        rank = (jnp.sum(jnp.cumsum(onehot, axis=0) * onehot, axis=1) - 1).astype(jnp.int32)
        hidden_buf = jnp.zeros((experts, group_cap, F_WIN), jnp.float32).at[id_rows, rank].set(hidden_rows.astype(jnp.float32))
        scaled_buf = jnp.zeros((experts, group_cap, D_WIN), jnp.float32).at[id_rows, rank].set(scaled_rows.astype(jnp.float32))
        out_buf = jnp.einsum('ecf,efd->ecd', hidden_buf, weight).astype(jnp.bfloat16)
        back_buf = jnp.einsum('ecd,efd->ecf', scaled_buf, weight).astype(jnp.bfloat16)
        term = jnp.einsum('ecf,ecd->efd', hidden_buf, scaled_buf).astype(jnp.bfloat16)
        term = lax.optimization_barrier(term).astype(jnp.float32)
        return total + term, (out_buf[id_rows, rank], back_buf[id_rows, rank])

    start = jnp.zeros((experts, F_WIN, D_WIN), jnp.float32)
    total, (out_rows, back_rows) = lax.scan(one_group, start, (hidden_groups, scaled_groups, id_groups))
    expert_out = ungroup(out_rows)
    hidden_grad = ungroup(back_rows)
    mixed = (gate_prob[:, None] * expert_out.astype(jnp.float32)).astype(jnp.bfloat16)
    code_grad = total * scales[:, :, None]
    return mixed, hidden_grad, code_grad
```

```python
import functools

import jax
import jax.numpy as jnp
from jax import lax
from jax.experimental import pallas as pl
from jax.experimental.pallas import tpu as pltpu
from jax.sharding import PartitionSpec as P

MESH = pl.DeviceIdType.MESH
BF = jnp.bfloat16
F32 = jnp.float32


def dot(a, b, dims):
    return lax.dot_general(a, b, (dims, ((), ())), preferred_element_type=F32)


def kernel(
    nl, nh, nx, ny,
    ids_ref, gate_ref, hid_ref, og_ref, codes_ref, scales_ref,
    mixed_ref, hg_ref, cg_ref,
    snd, rcv, ret_snd, ret_rcv, w1, wf, tsnd, g1, g2s, g2,
    d_ss, d_rs, r_ss, r_rs, w1_ss, w1_rs, w2_ss, w2_rs, g1_ss, g1_rs, g2_ss, g2_rs,
):
    ne = 2 * nx
    npl = ny * ne
    nz = nh * nl
    tok, fdim = hid_ref.shape
    cap = snd.shape[1]
    fb = fdim // nl
    cb = codes_ref.shape[2]
    dc = nx * cb
    half = nl // 2 - 1

    zl = lax.axis_index("rep")
    node = lax.axis_index("node")
    shard = lax.axis_index("shard")
    h, c = node // 2, node % 2
    x, y = shard // ny, shard % ny
    z = h * nl + zl
    me = y * ne + x * 2 + c

    def dev(xx, yy, zz, cc):
        return (zz % nl, (zz // nl) * 2 + cc, xx * ny + yy)

    def plane(p):
        return dev((p % ne) // 2, p // ne, z, p % 2)

    def w2_delta(hh, dk):
        return dk - half - hh % 2

    def g1_delta(dk):
        return dk - half - c

    barrier = pltpu.get_barrier_semaphore()

    def signal(target):
        pl.semaphore_signal(barrier, inc=1, device_id=target, device_id_type=MESH)

    @pl.loop(1, npl)
    def _(k):
        signal(plane((me + k) % npl))

    @pl.loop(1, nh)
    def _(k):
        signal(dev(x, y, ((h + k) % nh) * nl + zl, c))

    @pl.loop(0, nx * nl)
    def _(i):
        xs, delta = i // nl, w2_delta(x, i % nl)

        @pl.when(jnp.logical_not((xs == x) & (delta == 0)))
        def _():
            signal(dev(xs, y, (z - delta + nz) % nz, c))

    @pl.loop(0, nl)
    def _(dk):
        delta = g1_delta(dk)

        @pl.when(delta != 0)
        def _():
            signal(dev(x, y, (z - delta + nz) % nz, c))

    @pl.loop(0, nh)
    def _(hs):
        @pl.when(jnp.logical_not((hs == h) & (x == h)))
        def _():
            signal(dev(h, y, hs * nl + zl, c))

    ids = ids_ref[...]
    erows = lax.broadcasted_iota(jnp.int32, (16, tok), 0)
    onehot = (erows == ids).astype(F32)
    ti = lax.broadcasted_iota(jnp.int32, (tok, tok), 0)
    tj = lax.broadcasted_iota(jnp.int32, (tok, tok), 1)
    upto = (ti <= tj).astype(BF)
    count = dot(onehot.astype(BF), upto, ((1,), (0,)))
    rank = jnp.sum(count * onehot, axis=0, keepdims=True) - 1.0
    target = ids * cap + rank.astype(jnp.int32)
    slots = lax.broadcasted_iota(jnp.int32, (ne * cap, tok), 0)
    placing = (slots == target).astype(BF)
    gate = jnp.sum(jnp.where(ti == tj, gate_ref[...], 0.0), axis=1, keepdims=True)

    fi = lax.broadcasted_iota(jnp.int32, (fb, fdim), 0) + zl * fb
    fj = lax.broadcasted_iota(jnp.int32, (fb, fdim), 1)
    scale = jnp.sum(jnp.where(fi == fj, scales_ref[...], 0.0), axis=1, keepdims=True)
    frow = pl.multiple_of(zl * fb, fb)
    block = codes_ref[0, pl.ds(frow, fb), :].astype(F32) * scale
    w1[h] = block.astype(BF)

    pl.semaphore_wait(
        barrier,
        (npl - 1) + (nh - 1) + (nx * nl - 1) + (nl - 1) + nh - jnp.where(x == h, 1, 0),
    )

    def w1_copy(k, slot):
        return pltpu.make_async_remote_copy(
            src_ref=w1.at[slot], dst_ref=w1.at[slot],
            send_sem=w1_ss.at[k], recv_sem=w1_rs.at[slot],
            device_id=dev(x, y, ((h + k) % nh) * nl + zl, c), device_id_type=MESH,
        )

    @pl.loop(1, nh)
    def _(k):
        w1_copy(k, h).start()

    hid_rows = dot(placing, hid_ref[...], ((1,), (0,))).astype(BF).reshape(ne, cap, fdim)
    for yy in range(ny):
        snd[yy * ne:(yy + 1) * ne, :, 0:fdim] = hid_rows
    for yy in range(ny):
        for xx in range(nx):
            s0 = (xx * ny + yy) * cb
            cols = (gate * og_ref[:, s0:s0 + cb].astype(F32)).astype(BF)
            rows = dot(placing, cols, ((1,), (0,))).astype(BF).reshape(ne, cap, cb)
            snd[yy * ne:(yy + 1) * ne, :, fdim + xx * cb:fdim + (xx + 1) * cb] = rows
    rcv[me] = snd[me]

    def d_copy(p, slot):
        return pltpu.make_async_remote_copy(
            src_ref=snd.at[p], dst_ref=rcv.at[slot],
            send_sem=d_ss.at[p], recv_sem=d_rs.at[slot],
            device_id=plane(p), device_id_type=MESH,
        )

    @pl.loop(1, npl)
    def _(k):
        d_copy((me + k) % npl, me).start()

    @pl.loop(1, nh)
    def _(k):
        w1_copy(k, (h + k) % nh).wait_recv()

    wf[pl.ds(frow, fb), pl.ds(pl.multiple_of(x * cb, cb), cb)] = w1[x]

    def w2_copy(hh, delta, fblk, xcol, sem_i, sem_r):
        return pltpu.make_async_remote_copy(
            src_ref=w1.at[hh],
            dst_ref=wf.at[
                pl.ds(pl.multiple_of(fblk * fb, fb), fb), pl.ds(pl.multiple_of(xcol * cb, cb), cb)
            ],
            send_sem=w2_ss.at[sem_i], recv_sem=w2_rs.at[sem_r],
            device_id=dev(hh, y, (z + delta + nz) % nz, c), device_id_type=MESH,
        )

    def w2_not_self(i):
        hh = i // nl
        return jnp.logical_not((hh == x) & (w2_delta(hh, i % nl) == 0))

    @pl.loop(0, nx * nl)
    def _(i):
        @pl.when(w2_not_self(i))
        def _():
            hh = i // nl
            w2_copy(hh, w2_delta(hh, i % nl), zl, x, i, x * nl + zl).start()

    @pl.loop(1, npl)
    def _(k):
        p = (me + k) % npl
        d_copy(p, p).wait_recv()

    sc_all = rcv[:, :, fdim:fdim + dc].reshape(npl * cap, dc)
    fchunk = fdim // 2
    for k in range(2):
        hid_c = rcv[:, :, k * fchunk:(k + 1) * fchunk].reshape(npl * cap, fchunk)
        t = dot(hid_c, sc_all, ((0,), (0,))).astype(BF)
        tsnd[k * (nl // 2):(k + 1) * (nl // 2)] = t.reshape(nl // 2, fb, dc)

    def g1_copy(dk):
        delta = g1_delta(dk)
        return pltpu.make_async_remote_copy(
            src_ref=tsnd.at[(zl + delta + nl) % nl], dst_ref=g1.at[dk],
            send_sem=g1_ss.at[dk], recv_sem=g1_rs.at[dk],
            device_id=dev(x, y, (z + delta + nz) % nz, c), device_id_type=MESH,
        )

    @pl.loop(0, nl)
    def _(dk):
        @pl.when(g1_delta(dk) != 0)
        def _():
            g1_copy(dk).start()

    @pl.loop(0, nx * nl)
    def _(i):
        @pl.when(i != x * nl + zl)
        def _():
            w2_copy(0, 0, i % nl, i // nl, i, i).wait_recv()

    def r_copy(p, slot):
        return pltpu.make_async_remote_copy(
            src_ref=ret_snd.at[p], dst_ref=ret_rcv.at[slot],
            send_sem=r_ss.at[p], recv_sem=r_rs.at[slot],
            device_id=plane(p), device_id_type=MESH,
        )

    @pl.loop(0, ny)
    def _(k):
        p0 = ((y + k) % ny) * ne
        hid_c = rcv[pl.ds(p0, ne), :, 0:fdim].reshape(ne * cap, fdim)
        sc_c = rcv[pl.ds(p0, ne), :, fdim:fdim + dc].reshape(ne * cap, dc)
        o = dot(hid_c, wf[...], ((1,), (0,))).astype(BF)
        ret_snd[pl.ds(p0, ne), :, 0:dc] = o.reshape(ne, cap, dc)
        b = dot(sc_c, wf[...], ((1,), (1,))).astype(BF)
        ret_snd[pl.ds(p0, ne), :, dc:dc + fdim] = b.reshape(ne, cap, fdim)

        @pl.loop(0, ne)
        def _(i):
            p = p0 + (me + i) % ne

            @pl.when(p != me)
            def _():
                r_copy(p, me).start()

    ret_rcv[me] = ret_snd[me]

    @pl.loop(0, nl)
    def _(dk):
        @pl.when(g1_delta(dk) != 0)
        def _():
            g1_copy(dk).wait_recv()

    g1[half + c] = tsnd[zl]
    for j in range(nx):
        part = g1[0, :, j * cb:(j + 1) * cb].astype(F32)
        for dk in range(1, nl):
            part = part + g1[dk, :, j * cb:(j + 1) * cb].astype(F32)
        g2s[j] = part.astype(BF)

    def g2_copy(j, slot):
        return pltpu.make_async_remote_copy(
            src_ref=g2s.at[j], dst_ref=g2.at[slot],
            send_sem=g2_ss.at[j], recv_sem=g2_rs.at[slot],
            device_id=dev(j, y, x * nl + zl, c), device_id_type=MESH,
        )

    @pl.loop(0, nx)
    def _(j):
        @pl.when(jnp.logical_not((j == x) & (x == h)))
        def _():
            g2_copy(j, h).start()

    @pl.when(x == h)
    def _():
        g2[h] = g2s[x]

    @pl.loop(1, npl)
    def _(k):
        p = (me + k) % npl
        r_copy(p, p).wait_recv()

    back = None
    for yy in range(ny):
        rows = ret_rcv[yy * ne:(yy + 1) * ne, :, 0:dc].reshape(ne * cap, dc)
        token_out = gate * dot(placing, rows, ((0,), (0,)))
        for xx in range(nx):
            s0 = (xx * ny + yy) * cb
            mixed_ref[:, s0:s0 + cb] = token_out[:, xx * cb:(xx + 1) * cb].astype(BF)
        part = ret_rcv[yy * ne:(yy + 1) * ne, :, dc:dc + fdim].astype(F32)
        back = part if back is None else back + part
    back = back.reshape(ne * cap, fdim).astype(BF)
    hg_ref[...] = dot(placing, back, ((0,), (0,))).astype(BF)

    @pl.loop(0, nh)
    def _(hs):
        @pl.when(jnp.logical_not((hs == h) & (x == h)))
        def _():
            g2_copy(0, hs).wait_recv()

    total = g2[0].astype(F32)
    for hs in range(1, nh):
        total = total + g2[hs].astype(F32)
    cg_ref[0] = total * scale

    @pl.loop(1, nh)
    def _(k):
        w1_copy(k, h).wait_send()

    @pl.loop(1, npl)
    def _(k):
        p = (me + k) % npl
        d_copy(p, me).wait_send()
        r_copy(p, me).wait_send()

    @pl.loop(0, nx * nl)
    def _(i):
        @pl.when(w2_not_self(i))
        def _():
            w2_copy(0, 0, 0, 0, i, 0).wait_send()

    @pl.loop(0, nl)
    def _(dk):
        @pl.when(g1_delta(dk) != 0)
        def _():
            g1_copy(dk).wait_send()

    @pl.loop(0, nx)
    def _(j):
        @pl.when(jnp.logical_not((j == x) & (x == h)))
        def _():
            g2_copy(j, h).wait_send()


def body(nl, nh, nx, ny, hidden_in, expert_ids, gate_prob, out_grad, codes, scales):
    tok, fdim = hidden_in.shape
    ddim = out_grad.shape[1]
    cb = codes.shape[2]
    dc = nx * cb
    ne = 2 * nx
    npl = ny * ne
    cap = 3 * tok // (2 * ne)
    fb = fdim // nl
    dma = pltpu.SemaphoreType.DMA
    vmem = pl.BlockSpec(memory_space=pltpu.VMEM)
    return pl.pallas_call(
        functools.partial(kernel, nl, nh, nx, ny),
        out_shape=(
            jax.ShapeDtypeStruct((tok, ddim), BF),
            jax.ShapeDtypeStruct((tok, fdim), BF),
            jax.ShapeDtypeStruct((1, fb, cb), F32),
        ),
        in_specs=[vmem] * 6,
        out_specs=(vmem,) * 3,
        scratch_shapes=[
            pltpu.VMEM((npl, cap, fdim + dc), BF),
            pltpu.VMEM((npl, cap, fdim + dc), BF),
            pltpu.VMEM((npl, cap, fdim + dc), BF),
            pltpu.VMEM((npl, cap, fdim + dc), BF),
            pltpu.VMEM((nh, fb, cb), BF),
            pltpu.VMEM((fdim, dc), BF),
            pltpu.VMEM((nl, fb, dc), BF),
            pltpu.VMEM((nl, fb, dc), BF),
            pltpu.VMEM((nx, fb, cb), BF),
            pltpu.VMEM((nh, fb, cb), BF),
            dma((npl,)), dma((npl,)), dma((npl,)), dma((npl,)),
            dma((nh,)), dma((nh,)), dma((nx * nl,)), dma((nx * nl,)),
            dma((nl,)), dma((nl,)), dma((nx,)), dma((nh,)),
        ],
        compiler_params=pltpu.CompilerParams(
            collective_id=0, has_side_effects=True, vmem_limit_bytes=50 * 2**20
        ),
        cost_estimate=pl.CostEstimate(
            flops=6 * npl * cap * fdim * dc, bytes_accessed=4 * tok * ddim, transcendentals=0
        ),
    )(
        expert_ids.reshape(1, tok), gate_prob.reshape(1, tok), hidden_in, out_grad, codes, scales
    )


def solution(mesh):
    nl, nh = mesh.shape["rep"], mesh.shape["node"] // 2
    nx = nh
    ny = mesh.shape["shard"] // nx
    return jax.shard_map(
        functools.partial(body, nl, nh, nx, ny),
        mesh=mesh,
        in_specs=(
            P(("rep", "node", "shard"), None),
            P(("rep", "node", "shard"), None),
            P(("rep", "node", "shard")),
            P(("rep", "node", "shard"), None),
            P("node", None, "shard"),
            P("node", None),
        ),
        out_specs=(
            P(("rep", "node", "shard"), None),
            P(("rep", "node", "shard"), None),
            P("node", "rep", "shard"),
        ),
        check_vma=False,
    )
```

```python
import functools

import jax
import jax.numpy as jnp
from jax import lax
from jax.experimental import pallas as pl
from jax.experimental.pallas import tpu as pltpu
from jax.sharding import PartitionSpec as P

MESH = pl.DeviceIdType.MESH
BF = jnp.bfloat16
F32 = jnp.float32


def dot(a, b, dims):
    return lax.dot_general(a, b, (dims, ((), ())), preferred_element_type=F32)


def kernel(
    nl, nh, nx, ny,
    ids_ref, gate_ref, hid_hbm, og_hbm, codes_hbm, scales_ref,
    mixed_ref, hg_ref, cg_ref,
    hid_ref, og_ref, codes_ref,
    snd, rcv, ret_snd, ret_rcv, xb_snd, xb_rcv, w1, wf, tsnd, g1, g2s, ga, gb,
    in_s, d_ss, d_rs, f_ss, f_rs, r_ss, r_rs, x_ss, x_rs,
    w1_ss, w1_rs, w2_ss, w2_rs, g1_ss, g1_rs, ga_ss, ga_rs, gb_ss, gb_rs,
):
    ne = 2 * nx
    npl = ny * ne
    nsame = npl // 2
    nq = ny // 2
    nz = nh * nl
    tok, fdim = hid_ref.shape
    cap = snd.shape[1]
    fb, cb = codes_ref.shape
    dc = nx * cb
    half = nl // 2 - 1

    zl = lax.axis_index("rep")
    node = lax.axis_index("node")
    shard = lax.axis_index("shard")
    h, c = node // 2, node % 2
    x, y = shard // ny, shard % ny
    z = h * nl + zl
    quarter = (y // 2) * 2 + c
    me = quarter * ne + x * 2 + y % 2
    me_same = (quarter // 2) * ne + x * 2 + y % 2
    ty, tc = (y // 2) * 2 + c, y % 2
    untwisted = y % 2 == c

    def dev(xx, yy, zz, cc):
        return (zz % nl, (zz // nl) * 2 + cc, xx * ny + yy)

    def plane(p):
        q, e = p // ne, p % ne
        return dev(e // 2, (q // 2) * 2 + e % 2, z, q % 2)

    def of_core(i, core):
        return ((i // ne) * 2 + core) * ne + i % ne

    def w2_delta(hh, dk):
        return dk - half - hh % 2

    def g1_delta(dk):
        return dk - half - c

    frow = pl.multiple_of(zl * fb, fb)
    loads = (
        pltpu.make_async_copy(codes_hbm.at[0, pl.ds(frow, fb)], codes_ref, in_s.at[0]),
        pltpu.make_async_copy(hid_hbm, hid_ref, in_s.at[1]),
        pltpu.make_async_copy(og_hbm, og_ref, in_s.at[2]),
    )
    for load in loads:
        load.start()

    barrier = pltpu.get_barrier_semaphore()

    def signal(target):
        pl.semaphore_signal(barrier, inc=1, device_id=target, device_id_type=MESH)

    def w2_self(hh, delta):
        return (hh == x) & untwisted & (delta == 0)

    @pl.loop(1, npl)
    def _(k):
        signal(plane((me + k) % npl))

    @pl.loop(1, nh)
    def _(k):
        signal(dev(x, y, ((h + k) % nh) * nl + zl, c))

    @pl.loop(0, nx * nl)
    def _(i):
        xs, delta = i // nl, w2_delta(x, i % nl)

        @pl.when(jnp.logical_not(w2_self(xs, delta)))
        def _():
            signal(dev(xs, ty, (z - delta + nz) % nz, tc))

    @pl.loop(0, nl)
    def _(dk):
        delta = g1_delta(dk)

        @pl.when(delta != 0)
        def _():
            signal(dev(x, y, (z - delta + nz) % nz, c))

    ids = ids_ref[...]
    erows = lax.broadcasted_iota(jnp.int32, (16, tok), 0)
    onehot = (erows == ids).astype(F32)
    ti = lax.broadcasted_iota(jnp.int32, (tok, tok), 0)
    tj = lax.broadcasted_iota(jnp.int32, (tok, tok), 1)
    upto = (ti <= tj).astype(BF)
    count = dot(onehot.astype(BF), upto, ((1,), (0,)))
    rank = jnp.sum(count * onehot, axis=0, keepdims=True) - 1.0
    target = ids * cap + rank.astype(jnp.int32)
    slots = lax.broadcasted_iota(jnp.int32, (ne * cap, tok), 0)
    placing = (slots == target).astype(BF)
    gate = jnp.sum(jnp.where(ti == tj, gate_ref[...], 0.0), axis=1, keepdims=True)

    fi = lax.broadcasted_iota(jnp.int32, (fb, fdim), 0) + zl * fb
    fj = lax.broadcasted_iota(jnp.int32, (fb, fdim), 1)
    scale = jnp.sum(jnp.where(fi == fj, scales_ref[...], 0.0), axis=1, keepdims=True)
    loads[0].wait()
    w1[h] = (codes_ref[...].astype(F32) * scale).astype(BF)

    loads[1].wait()
    hid_rows = dot(placing, hid_ref[...], ((1,), (0,))).astype(BF).reshape(ne, cap, fdim)
    for k in range(nq):
        snd[pl.ds((2 * k + c) * ne, ne), :, 0:fdim] = hid_rows
    loads[2].wait()
    for q in range(ny):
        for xx in range(nx):
            s0 = (xx * ny + q) * cb
            cols = (gate * og_ref[:, s0:s0 + cb].astype(F32)).astype(BF)
            rows = dot(placing, cols, ((1,), (0,))).astype(BF).reshape(ne, cap, cb)
            snd[q * ne:(q + 1) * ne, :, fdim + xx * cb:fdim + (xx + 1) * cb] = rows
    rcv[me] = snd[me]

    pl.semaphore_wait(
        barrier,
        (npl - 1) + (nh - 1) + (nx * nl - jnp.where(untwisted, 1, 0)) + (nl - 1),
    )

    def w1_copy(k, slot):
        return pltpu.make_async_remote_copy(
            src_ref=w1.at[slot], dst_ref=w1.at[slot],
            send_sem=w1_ss.at[k], recv_sem=w1_rs.at[slot],
            device_id=dev(x, y, ((h + k) % nh) * nl + zl, c), device_id_type=MESH,
        )

    @pl.loop(1, nh)
    def _(k):
        w1_copy(k, h).start()

    def d_whole(p, slot):
        return pltpu.make_async_remote_copy(
            src_ref=snd.at[p], dst_ref=rcv.at[slot],
            send_sem=d_ss.at[p], recv_sem=d_rs.at[slot],
            device_id=plane(p), device_id_type=MESH,
        )

    def d_scaled(p, slot):
        return pltpu.make_async_remote_copy(
            src_ref=snd.at[p, :, pl.ds(fdim, dc)], dst_ref=rcv.at[slot, :, pl.ds(fdim, dc)],
            send_sem=d_ss.at[p], recv_sem=d_rs.at[slot],
            device_id=plane(p), device_id_type=MESH,
        )

    def d_forward(i, slot):
        return pltpu.make_async_remote_copy(
            src_ref=rcv.at[slot, :, pl.ds(0, fdim)], dst_ref=rcv.at[slot, :, pl.ds(0, fdim)],
            send_sem=f_ss.at[i], recv_sem=f_rs.at[i],
            device_id=dev(x, y, z, 1 - c), device_id_type=MESH,
        )

    d_forward(me_same, me).start()

    @pl.loop(1, nsame)
    def _(k):
        d_whole(of_core((me_same + k) % nsame, c), me).start()

    @pl.loop(0, nsame)
    def _(k):
        d_scaled(of_core((me_same + k) % nsame, 1 - c), me).start()

    @pl.loop(1, nh)
    def _(k):
        w1_copy(k, (h + k) % nh).wait_recv()

    @pl.when(untwisted)
    def _():
        wf[pl.ds(frow, fb), pl.ds(pl.multiple_of(x * cb, cb), cb)] = w1[x]

    def w2_copy(hh, delta, fblk, xcol, sem_i, sem_r):
        return pltpu.make_async_remote_copy(
            src_ref=w1.at[hh],
            dst_ref=wf.at[
                pl.ds(pl.multiple_of(fblk * fb, fb), fb), pl.ds(pl.multiple_of(xcol * cb, cb), cb)
            ],
            send_sem=w2_ss.at[sem_i], recv_sem=w2_rs.at[sem_r],
            device_id=dev(hh, ty, (z + delta + nz) % nz, tc), device_id_type=MESH,
        )

    @pl.loop(0, nx * nl)
    def _(i):
        hh, delta = i // nl, w2_delta(i // nl, i % nl)

        @pl.when(jnp.logical_not(w2_self(hh, delta)))
        def _():
            w2_copy(hh, delta, zl, x, i, x * nl + zl).start()

    @pl.loop(1, nsame)
    def _(k):
        i = (me_same - k + nsame) % nsame
        p = of_core(i, c)
        d_whole(p, p).wait_recv()
        d_forward(i, p).start()

    @pl.loop(0, nsame)
    def _(k):
        p = of_core((me_same - k + nsame) % nsame, 1 - c)
        d_scaled(p, p).wait_recv()

    @pl.loop(0, nsame)
    def _(i):
        d_forward(i, of_core(i, 1 - c)).wait_recv()

    sc_all = rcv[:, :, fdim:fdim + dc].reshape(npl * cap, dc)
    fchunk = fdim // 2
    for k in range(2):
        hid_c = rcv[:, :, k * fchunk:(k + 1) * fchunk].reshape(npl * cap, fchunk)
        t = dot(hid_c, sc_all, ((0,), (0,))).astype(BF)
        tsnd[k * (nl // 2):(k + 1) * (nl // 2)] = t.reshape(nl // 2, fb, dc)

    def g1_copy(dk):
        delta = g1_delta(dk)
        return pltpu.make_async_remote_copy(
            src_ref=tsnd.at[(zl + delta + nl) % nl], dst_ref=g1.at[dk],
            send_sem=g1_ss.at[dk], recv_sem=g1_rs.at[dk],
            device_id=dev(x, y, (z + delta + nz) % nz, c), device_id_type=MESH,
        )

    @pl.loop(0, nl)
    def _(dk):
        @pl.when(g1_delta(dk) != 0)
        def _():
            g1_copy(dk).start()

    @pl.loop(0, nx * nl)
    def _(i):
        @pl.when(jnp.logical_not(untwisted & (i == x * nl + zl)))
        def _():
            w2_copy(0, 0, i % nl, i // nl, i, i).wait_recv()

    def x_copy(k):
        return pltpu.make_async_remote_copy(
            src_ref=xb_snd.at[k], dst_ref=xb_rcv.at[k],
            send_sem=x_ss.at[k], recv_sem=x_rs.at[k],
            device_id=dev(x, y, z, 1 - c), device_id_type=MESH,
        )

    def r_whole(p, slot):
        return pltpu.make_async_remote_copy(
            src_ref=ret_snd.at[p], dst_ref=ret_rcv.at[slot],
            send_sem=r_ss.at[p], recv_sem=r_rs.at[slot],
            device_id=plane(p), device_id_type=MESH,
        )

    def r_out(p, slot):
        return pltpu.make_async_remote_copy(
            src_ref=ret_snd.at[p, :, pl.ds(0, dc)], dst_ref=ret_rcv.at[slot, :, pl.ds(0, dc)],
            send_sem=r_ss.at[p], recv_sem=r_rs.at[slot],
            device_id=plane(p), device_id_type=MESH,
        )

    @pl.loop(0, nq)
    def _(k):
        p0 = (2 * k + 1 - c) * ne
        sc_c = rcv[pl.ds(p0, ne), :, fdim:fdim + dc].reshape(ne * cap, dc)
        b = dot(sc_c, wf[...], ((1,), (1,))).astype(BF)
        xb_snd[k] = b.reshape(ne, cap, fdim)
        x_copy(k).start()
        hid_c = rcv[pl.ds(p0, ne), :, 0:fdim].reshape(ne * cap, fdim)
        o = dot(hid_c, wf[...], ((1,), (0,))).astype(BF)
        ret_snd[pl.ds(p0, ne), :, 0:dc] = o.reshape(ne, cap, dc)

        @pl.loop(0, ne)
        def _(i):
            r_out(p0 + (me + i) % ne, me).start()

    @pl.loop(0, nq)
    def _(k):
        p0 = (2 * k + c) * ne
        hid_c = rcv[pl.ds(p0, ne), :, 0:fdim].reshape(ne * cap, fdim)
        sc_c = rcv[pl.ds(p0, ne), :, fdim:fdim + dc].reshape(ne * cap, dc)
        o = dot(hid_c, wf[...], ((1,), (0,))).astype(BF)
        ret_snd[pl.ds(p0, ne), :, 0:dc] = o.reshape(ne, cap, dc)
        b = dot(sc_c, wf[...], ((1,), (1,)))
        x_copy(k).wait_recv()
        b = b.reshape(ne, cap, fdim) + xb_rcv[k].astype(F32)
        ret_snd[pl.ds(p0, ne), :, dc:dc + fdim] = b.astype(BF)

        @pl.loop(0, ne)
        def _(i):
            p = p0 + (me + i) % ne

            @pl.when(p != me)
            def _():
                r_whole(p, me).start()

    ret_rcv[me] = ret_snd[me]

    @pl.loop(0, nl)
    def _(dk):
        @pl.when(g1_delta(dk) != 0)
        def _():
            g1_copy(dk).wait_recv()

    g1[half + c] = tsnd[zl]
    for j in range(nx):
        part = g1[0, :, j * cb:(j + 1) * cb].astype(F32)
        for dk in range(1, nl):
            part = part + g1[dk, :, j * cb:(j + 1) * cb].astype(F32)
        g2s[j] = part.astype(BF)

    def ga_copy(j, slot):
        return pltpu.make_async_remote_copy(
            src_ref=g2s.at[j], dst_ref=ga.at[slot],
            send_sem=ga_ss.at[j], recv_sem=ga_rs.at[slot],
            device_id=dev(j, ty, z, tc), device_id_type=MESH,
        )

    def gb_copy(j, slot):
        return pltpu.make_async_remote_copy(
            src_ref=ga.at[j], dst_ref=gb.at[slot],
            send_sem=gb_ss.at[j], recv_sem=gb_rs.at[slot],
            device_id=dev(x, y, j * nl + zl, c), device_id_type=MESH,
        )

    @pl.loop(0, nx)
    def _(j):
        @pl.when(jnp.logical_not((j == x) & untwisted))
        def _():
            ga_copy(j, x).start()

    @pl.when(untwisted)
    def _():
        ga[x] = g2s[x]

    @pl.loop(0, nx)
    def _(j):
        @pl.when(jnp.logical_not((j == x) & untwisted))
        def _():
            ga_copy(j, j).wait_recv()

        @pl.when(j != h)
        def _():
            gb_copy(j, h).start()

    gb[h] = ga[h]

    @pl.loop(0, nsame)
    def _(k):
        p = of_core((me_same - k + nsame) % nsame, 1 - c)
        r_out(p, p).wait_recv()

    @pl.loop(1, nsame)
    def _(k):
        p = of_core((me_same - k + nsame) % nsame, c)
        r_whole(p, p).wait_recv()

    for q in range(ny):
        rows = ret_rcv[q * ne:(q + 1) * ne, :, 0:dc].reshape(ne * cap, dc)
        token_out = gate * dot(placing, rows, ((0,), (0,)))
        for xx in range(nx):
            s0 = (xx * ny + q) * cb
            mixed_ref[:, s0:s0 + cb] = token_out[:, xx * cb:(xx + 1) * cb].astype(BF)
    back = ret_rcv[pl.ds(c * ne, ne), :, dc:dc + fdim].astype(F32)
    for k in range(1, nq):
        back = back + ret_rcv[pl.ds((2 * k + c) * ne, ne), :, dc:dc + fdim].astype(F32)
    back = back.reshape(ne * cap, fdim).astype(BF)
    hg_ref[...] = dot(placing, back, ((0,), (0,))).astype(BF)

    @pl.loop(0, nh)
    def _(hs):
        @pl.when(hs != h)
        def _():
            gb_copy(0, hs).wait_recv()

    total = gb[0].astype(F32)
    for hs in range(1, nh):
        total = total + gb[hs].astype(F32)
    cg_ref[0] = total * scale

    @pl.loop(1, nh)
    def _(k):
        w1_copy(k, h).wait_send()

    @pl.loop(0, nsame)
    def _(i):
        p, far = of_core(i, c), of_core(i, 1 - c)
        d_forward(i, p).wait_send()
        d_scaled(far, me).wait_send()
        r_out(far, me).wait_send()

        @pl.when(p != me)
        def _():
            d_whole(p, me).wait_send()
            r_whole(p, me).wait_send()

    @pl.loop(0, nq)
    def _(k):
        x_copy(k).wait_send()

    @pl.loop(0, nx * nl)
    def _(i):
        @pl.when(jnp.logical_not(w2_self(i // nl, w2_delta(i // nl, i % nl))))
        def _():
            w2_copy(0, 0, 0, 0, i, 0).wait_send()

    @pl.loop(0, nl)
    def _(dk):
        @pl.when(g1_delta(dk) != 0)
        def _():
            g1_copy(dk).wait_send()

    @pl.loop(0, nx)
    def _(j):
        @pl.when(jnp.logical_not((j == x) & untwisted))
        def _():
            ga_copy(j, x).wait_send()

        @pl.when(j != h)
        def _():
            gb_copy(j, h).wait_send()


def body(nl, nh, nx, ny, hidden_in, expert_ids, gate_prob, out_grad, codes, scales):
    tok, fdim = hidden_in.shape
    ddim = out_grad.shape[1]
    cb = codes.shape[2]
    dc = nx * cb
    ne = 2 * nx
    npl = ny * ne
    cap = 3 * tok // (2 * ne)
    fb = fdim // nl
    dma = pltpu.SemaphoreType.DMA
    vmem = pl.BlockSpec(memory_space=pltpu.VMEM)
    hbm = pl.BlockSpec(memory_space=pl.ANY)
    return pl.pallas_call(
        functools.partial(kernel, nl, nh, nx, ny),
        out_shape=(
            jax.ShapeDtypeStruct((tok, ddim), BF),
            jax.ShapeDtypeStruct((tok, fdim), BF),
            jax.ShapeDtypeStruct((1, fb, cb), F32),
        ),
        in_specs=[vmem, vmem, hbm, hbm, hbm, vmem],
        out_specs=(vmem,) * 3,
        scratch_shapes=[
            pltpu.VMEM((tok, fdim), BF),
            pltpu.VMEM((tok, ddim), BF),
            pltpu.VMEM((fb, cb), BF),
            pltpu.VMEM((npl, cap, fdim + dc), BF),
            pltpu.VMEM((npl, cap, fdim + dc), BF),
            pltpu.VMEM((npl, cap, fdim + dc), BF),
            pltpu.VMEM((npl, cap, fdim + dc), BF),
            pltpu.VMEM((ny // 2, ne, cap, fdim), BF),
            pltpu.VMEM((ny // 2, ne, cap, fdim), BF),
            pltpu.VMEM((nh, fb, cb), BF),
            pltpu.VMEM((fdim, dc), BF),
            pltpu.VMEM((nl, fb, dc), BF),
            pltpu.VMEM((nl, fb, dc), BF),
            pltpu.VMEM((nx, fb, cb), BF),
            pltpu.VMEM((nx, fb, cb), BF),
            pltpu.VMEM((nh, fb, cb), BF),
            dma((3,)), dma((npl,)), dma((npl,)), dma((npl // 2,)), dma((npl // 2,)),
            dma((npl,)), dma((npl,)), dma((ny // 2,)), dma((ny // 2,)),
            dma((nh,)), dma((nh,)), dma((nx * nl,)), dma((nx * nl,)),
            dma((nl,)), dma((nl,)), dma((nx,)), dma((nx,)), dma((nx,)), dma((nh,)),
        ],
        compiler_params=pltpu.CompilerParams(
            collective_id=0, has_side_effects=True, vmem_limit_bytes=60 * 2**20
        ),
        cost_estimate=pl.CostEstimate(
            flops=6 * npl * cap * fdim * dc, bytes_accessed=4 * tok * ddim, transcendentals=0
        ),
    )(
        expert_ids.reshape(1, tok), gate_prob.reshape(1, tok), hidden_in, out_grad, codes, scales
    )


def solution(mesh):
    nl, nh = mesh.shape["rep"], mesh.shape["node"] // 2
    nx = nh
    ny = mesh.shape["shard"] // nx
    return jax.shard_map(
        functools.partial(body, nl, nh, nx, ny),
        mesh=mesh,
        in_specs=(
            P(("rep", "node", "shard"), None),
            P(("rep", "node", "shard"), None),
            P(("rep", "node", "shard")),
            P(("rep", "node", "shard"), None),
            P("node", None, "shard"),
            P("node", None),
        ),
        out_specs=(
            P(("rep", "node", "shard"), None),
            P(("rep", "node", "shard"), None),
            P("node", "rep", "shard"),
        ),
        check_vma=False,
    )
```

```python
import functools

import jax
import jax.numpy as jnp
from jax import lax
from jax.experimental import pallas as pl
from jax.experimental.pallas import tpu as pltpu
from jax.sharding import PartitionSpec as P

MESH = pl.DeviceIdType.MESH
BF = jnp.bfloat16
F32 = jnp.float32


def dot(a, b, dims):
    return lax.dot_general(a, b, (dims, ((), ())), preferred_element_type=F32)


def div(a, b):
    return a // b if isinstance(a, int) else lax.div(a, b)


def rem(a, b):
    return a % b if isinstance(a, int) else lax.rem(a, b)


def kernel(
    nl, nh, nx, ny,
    ids_ref, gate_ref, hid_hbm, og_hbm, codes_hbm, scales_ref,
    mixed_ref, hg_ref, cg_ref,
    hid_ref, og_ref, codes_ref,
    snd, rcv, ret_snd, ret_rcv, xb_snd, xb_rcv, wown, w1, wf, tsnd, lng, sht, g2s, ga, gb,
    in_s, d_ss, d_rs, f_ss, f_rs, r_ss, r_rs, x_ss, x_rs,
    w1_ss, w1_rs, wo_ss, wo_rs, w2_ss, w2_rs, lg_ss, lg_rs, sh_ss, sh_rs, ga_ss, ga_rs, gb_ss, gb_rs,
):
    ne = 2 * nx
    npl = ny * ne
    nsame = div(npl, 2)
    nq = div(ny, 2)
    nz = nh * nl
    tok, fdim = hid_ref.shape
    cap = snd.shape[1]
    cb = codes_ref.shape[1]
    fb = div(fdim, nl)
    dc = nx * cb
    hc = div(dc, 2)
    steps = div(nl, 2)

    zl = lax.axis_index("rep")
    node = lax.axis_index("node")
    shard = lax.axis_index("shard")
    h, c = div(node, 2), rem(node, 2)
    x, y = div(shard, ny), rem(shard, ny)
    z = h * nl + zl
    quarter = div(y, 2) * 2 + c
    me = quarter * ne + x * 2 + rem(y, 2)
    me_same = div(quarter, 2) * ne + x * 2 + rem(y, 2)
    ty, tc = div(y, 2) * 2 + c, rem(y, 2)
    untwisted = rem(y, 2) == c

    def dev(xx, yy, zz, cc):
        return (rem(zz, nl), div(zz, nl) * 2 + cc, xx * ny + yy)

    sibling = dev(x, y, z, 1 - c)

    def plane(p):
        q, e = div(p, ne), rem(p, ne)
        return dev(div(e, 2), div(q, 2) * 2 + rem(e, 2), z, rem(q, 2))

    def of_core(i, core):
        return (div(i, ne) * 2 + core) * ne + rem(i, ne)

    def w2_delta(hh, dk):
        return dk - (div(nl, 2) - 1) - rem(hh, 2)

    def w1_turn(k):
        return (2 * c - 1) if 2 * k == nh else 0

    way = 1 - 2 * c

    frow = pl.multiple_of(zl * fb, fb)
    loads = (
        pltpu.make_async_copy(codes_hbm.at[0], codes_ref, in_s.at[0]),
        pltpu.make_async_copy(hid_hbm, hid_ref, in_s.at[1]),
        pltpu.make_async_copy(og_hbm, og_ref, in_s.at[2]),
    )
    for load in loads:
        load.start()

    barrier = pltpu.get_barrier_semaphore()

    def signal(target):
        pl.semaphore_signal(barrier, inc=1, device_id=target, device_id_type=MESH)

    def w2_self(hh, delta):
        return (hh == x) & untwisted & (delta == 0)

    @pl.loop(1, npl)
    def _(k):
        signal(plane(rem(me + k, npl)))

    for k in range(1, nh):
        signal(dev(x, y, rem(h - k + nh, nh) * nl + rem(zl - w1_turn(k) + nl, nl), c))
        signal(dev(x, y, rem(h + k, nh) * nl + zl, c))

    @pl.loop(0, nx * nl)
    def _(i):
        xs, delta = div(i, nl), w2_delta(x, rem(i, nl))

        @pl.when(jnp.logical_not(w2_self(xs, delta)))
        def _():
            signal(dev(xs, ty, rem(z - delta + nz, nz), tc))

    signal(dev(x, y, rem(z + 1, nz), c))
    signal(dev(x, y, rem(z - 1 + nz, nz), c))

    ids = ids_ref[...]
    erows = lax.broadcasted_iota(jnp.int32, (16, tok), 0)
    onehot = (erows == ids).astype(F32)
    ti = lax.broadcasted_iota(jnp.int32, (tok, tok), 0)
    tj = lax.broadcasted_iota(jnp.int32, (tok, tok), 1)
    upto = (ti <= tj).astype(BF)
    count = dot(onehot.astype(BF), upto, ((1,), (0,)))
    rank = jnp.sum(count * onehot, axis=0, keepdims=True) - 1.0
    target = ids * cap + rank.astype(jnp.int32)
    slots = lax.broadcasted_iota(jnp.int32, (ne * cap, tok), 0)
    placing = (slots == target).astype(BF)
    gate = jnp.sum(jnp.where(ti == tj, gate_ref[...], 0.0), axis=1, keepdims=True)

    fi = lax.broadcasted_iota(jnp.int32, (fb, fdim), 0) + zl * fb
    fj = lax.broadcasted_iota(jnp.int32, (fb, fdim), 1)
    scale = jnp.sum(jnp.where(fi == fj, scales_ref[...], 0.0), axis=1, keepdims=True)
    loads[0].wait()
    wide = min(128, fdim)
    eye_r = lax.broadcasted_iota(jnp.int32, (wide, wide), 0)
    eye_c = lax.broadcasted_iota(jnp.int32, (wide, wide), 1)
    for f0 in range(0, fdim, wide):
        col = jnp.where(eye_r == eye_c, scales_ref[:, f0:f0 + wide], 0.0)
        col = jnp.sum(col, axis=1, keepdims=True)
        wown[f0:f0 + wide] = (codes_ref[f0:f0 + wide].astype(F32) * col).astype(BF)
    w1[h] = wown[pl.ds(frow, fb)]

    loads[1].wait()
    hid_rows = dot(placing, hid_ref[...], ((1,), (0,))).astype(BF).reshape(ne, cap, fdim)
    for k in range(nq):
        snd[pl.ds((2 * k + c) * ne, ne), :, 0:fdim] = hid_rows
    loads[2].wait()
    for q in range(ny):
        for xx in range(nx):
            s0 = (xx * ny + q) * cb
            cols = (gate * og_ref[:, s0:s0 + cb].astype(F32)).astype(BF)
            rows = dot(placing, cols, ((1,), (0,))).astype(BF).reshape(ne, cap, cb)
            snd[q * ne:(q + 1) * ne, :, fdim + xx * cb:fdim + (xx + 1) * cb] = rows
    rcv[me] = snd[me]

    pl.semaphore_wait(
        barrier,
        (npl - 1) + 2 * (nh - 1) + (nx * nl - jnp.where(untwisted, 1, 0)) + 2,
    )

    def w1_copy(k, slot):
        row = rem(zl + w1_turn(k) + nl, nl)
        return pltpu.make_async_remote_copy(
            src_ref=wown.at[pl.ds(pl.multiple_of(row * fb, fb), fb)], dst_ref=w1.at[slot],
            send_sem=w1_ss.at[k], recv_sem=w1_rs.at[slot],
            device_id=dev(x, y, rem(h + k, nh) * nl + row, c), device_id_type=MESH,
        )

    def wo_copy(xcol):
        return pltpu.make_async_remote_copy(
            src_ref=wown, dst_ref=wf.at[:, pl.ds(pl.multiple_of(xcol * cb, cb), cb)],
            send_sem=wo_ss, recv_sem=wo_rs.at[xcol],
            device_id=dev(h, ty, z, tc), device_id_type=MESH,
        )

    near_first = sorted(range(1, nh), key=lambda k: -abs(2 * k - nh))
    for k in reversed(near_first):
        w1_copy(k, h).start()

    def d_whole(p, slot, target=None):
        return pltpu.make_async_remote_copy(
            src_ref=snd.at[p], dst_ref=rcv.at[slot],
            send_sem=d_ss.at[p], recv_sem=d_rs.at[slot],
            device_id=target or plane(p), device_id_type=MESH,
        )

    def d_scaled(p, slot, target=None):
        return pltpu.make_async_remote_copy(
            src_ref=snd.at[p, :, pl.ds(fdim, dc)], dst_ref=rcv.at[slot, :, pl.ds(fdim, dc)],
            send_sem=d_ss.at[p], recv_sem=d_rs.at[slot],
            device_id=target or plane(p), device_id_type=MESH,
        )

    def d_forward(i, slot):
        return pltpu.make_async_remote_copy(
            src_ref=rcv.at[slot, :, pl.ds(0, fdim)], dst_ref=rcv.at[slot, :, pl.ds(0, fdim)],
            send_sem=f_ss.at[i], recv_sem=f_rs.at[i],
            device_id=sibling, device_id_type=MESH,
        )

    d_forward(me_same, me).start()

    @pl.loop(1, nsame)
    def _(k):
        d_whole(of_core(rem(me_same + k, nsame), c), me).start()

    @pl.loop(0, nsame)
    def _(k):
        d_scaled(of_core(rem(me_same + k, nsame), 1 - c), me).start()

    @pl.when(jnp.logical_not((x == h) & untwisted))
    def _():
        wo_copy(x).start()

    @pl.when((x == h) & untwisted)
    def _():
        wf[:, pl.ds(pl.multiple_of(x * cb, cb), cb)] = wown[...]

    def w2_copy(hh, delta, fblk, xcol, sem_i, sem_r):
        return pltpu.make_async_remote_copy(
            src_ref=w1.at[hh],
            dst_ref=wf.at[
                pl.ds(pl.multiple_of(fblk * fb, fb), fb), pl.ds(pl.multiple_of(xcol * cb, cb), cb)
            ],
            send_sem=w2_ss.at[sem_i], recv_sem=w2_rs.at[sem_r],
            device_id=dev(hh, ty, rem(z + delta + nz, nz), tc), device_id_type=MESH,
        )

    def w2_sent(hh, delta):
        segment = div(rem(z + delta + nz, nz), nl)
        return (segment != hh) & jnp.logical_not(w2_self(hh, delta))

    def w2_send(hh):
        @pl.loop(0, nl)
        def _(dk):
            delta = w2_delta(hh, dk)

            @pl.when(w2_sent(hh, delta))
            def _():
                w2_copy(hh, delta, zl, x, hh * nl + dk, x * nl + zl).start()

    w2_send(h)
    for k in near_first:
        other = rem(h + nh - k, nh)
        w1_copy(k, other).wait_recv()
        w2_send(other)

    @pl.when((x != h) & untwisted)
    def _():
        wf[pl.ds(frow, fb), pl.ds(pl.multiple_of(x * cb, cb), cb)] = w1[x]

    @pl.loop(1, nsame)
    def _(k):
        i = rem(me_same - k + nsame, nsame)
        p = of_core(i, c)
        d_whole(p, p, sibling).wait_recv()
        d_forward(i, p).start()

    @pl.loop(0, nsame)
    def _(k):
        p = of_core(rem(me_same - k + nsame, nsame), 1 - c)
        d_scaled(p, p, sibling).wait_recv()

    @pl.loop(0, nsame)
    def _(i):
        d_forward(i, of_core(i, 1 - c)).wait_recv()

    def chain_copy(long, a, t):
        toward = way if long else -way
        d = (steps if long else steps - 1) - t
        slot, ss, rs = (lng, lg_ss, lg_rs) if long else (sht, sh_ss, sh_rs)
        return pltpu.make_async_remote_copy(
            src_ref=tsnd.at[a, rem(zl + toward * d + nl, nl)], dst_ref=slot.at[a, t],
            send_sem=ss.at[a, t], recv_sem=rs.at[a, t],
            device_id=dev(x, y, rem(z + toward + nz, nz), c), device_id_type=MESH,
        )

    def chain_step(t):
        for a in range(2):
            for long in (True, False):
                length = steps if long else steps - 1
                if t < length:
                    toward = way if long else -way
                    piece = rem(zl + toward * (length - t) + nl, nl)
                    slot = lng if long else sht
                    chain_copy(long, a, t - 1).wait_recv()
                    both = tsnd[a, piece].astype(F32) + slot[a, t - 1].astype(F32)
                    tsnd[a, piece] = both.astype(BF)
                    chain_copy(long, a, t).start()

    fchunk = div(fdim, 2)
    for a in range(2):
        lanes = slice(fdim + a * hc, fdim + (a + 1) * hc)
        sc_a = rcv[:, :, lanes].reshape(npl * cap, hc)
        for k in range(2):
            hid_c = rcv[:, :, k * fchunk:(k + 1) * fchunk].reshape(npl * cap, fchunk)
            t = dot(hid_c, sc_a, ((0,), (0,))).astype(BF)
            tsnd[a, k * div(nl, 2):(k + 1) * div(nl, 2)] = t.reshape(div(nl, 2), fb, hc)
        chain_copy(True, a, 0).start()
        if steps > 1:
            chain_copy(False, a, 0).start()

    def weights_arrived():
        @pl.when(x == h)
        def _():
            @pl.loop(0, nx)
            def _(i):
                @pl.when(jnp.logical_not(untwisted & (i == x)))
                def _():
                    wo_copy(i).wait_recv()

        @pl.when(x != h)
        def _():
            @pl.loop(0, nx * nl)
            def _(i):
                @pl.when(jnp.logical_not(untwisted & (i == x * nl + zl)))
                def _():
                    w2_copy(0, 0, rem(i, nl), div(i, nl), i, i).wait_recv()

    def x_copy(k):
        return pltpu.make_async_remote_copy(
            src_ref=xb_snd.at[k], dst_ref=xb_rcv.at[k],
            send_sem=x_ss.at[k], recv_sem=x_rs.at[k],
            device_id=sibling, device_id_type=MESH,
        )

    def r_whole(p, slot, target=None):
        return pltpu.make_async_remote_copy(
            src_ref=ret_snd.at[p], dst_ref=ret_rcv.at[slot],
            send_sem=r_ss.at[p], recv_sem=r_rs.at[slot],
            device_id=target or plane(p), device_id_type=MESH,
        )

    def r_out(p, slot, target=None):
        return pltpu.make_async_remote_copy(
            src_ref=ret_snd.at[p, :, pl.ds(0, dc)], dst_ref=ret_rcv.at[slot, :, pl.ds(0, dc)],
            send_sem=r_ss.at[p], recv_sem=r_rs.at[slot],
            device_id=target or plane(p), device_id_type=MESH,
        )

    def far_out(k):
        p0 = (2 * k + 1 - c) * ne
        hid_c = rcv[pl.ds(p0, ne), :, 0:fdim].reshape(ne * cap, fdim)
        o = dot(hid_c, wf[...], ((1,), (0,))).astype(BF)
        ret_snd[pl.ds(p0, ne), :, 0:dc] = o.reshape(ne, cap, dc)

        @pl.loop(0, ne)
        def _(i):
            r_out(p0 + rem(me + i, ne), me).start()

    def far_back(k):
        p0 = (2 * k + 1 - c) * ne
        sc_c = rcv[pl.ds(p0, ne), :, fdim:fdim + dc].reshape(ne * cap, dc)
        b = dot(sc_c, wf[...], ((1,), (1,))).astype(BF)
        xb_snd[k] = b.reshape(ne, cap, fdim)
        x_copy(k).start()

    def near_rows(k):
        p0 = (2 * k + c) * ne
        hid_c = rcv[pl.ds(p0, ne), :, 0:fdim].reshape(ne * cap, fdim)
        sc_c = rcv[pl.ds(p0, ne), :, fdim:fdim + dc].reshape(ne * cap, dc)
        o = dot(hid_c, wf[...], ((1,), (0,))).astype(BF)
        ret_snd[pl.ds(p0, ne), :, 0:dc] = o.reshape(ne, cap, dc)
        b = dot(sc_c, wf[...], ((1,), (1,)))
        x_copy(k).wait_recv()
        b = b.reshape(ne, cap, fdim) + xb_rcv[k].astype(F32)
        ret_snd[pl.ds(p0, ne), :, dc:dc + fdim] = b.astype(BF)

        @pl.loop(0, ne)
        def _(i):
            p = p0 + rem(me + i, ne)

            @pl.when(p != me)
            def _():
                r_whole(p, me).start()

    def ga_copy(j, slot):
        return pltpu.make_async_remote_copy(
            src_ref=g2s.at[j], dst_ref=ga.at[slot],
            send_sem=ga_ss.at[j], recv_sem=ga_rs.at[slot],
            device_id=dev(j, ty, z, tc), device_id_type=MESH,
        )

    def gb_copy(j, slot):
        return pltpu.make_async_remote_copy(
            src_ref=ga.at[j], dst_ref=gb.at[slot],
            send_sem=gb_ss.at[j], recv_sem=gb_rs.at[slot],
            device_id=dev(x, y, j * nl + zl, c), device_id_type=MESH,
        )

    def chain_end():
        for a in range(2):
            total = tsnd[a, zl].astype(F32)
            chain_copy(True, a, steps - 1).wait_recv()
            total = total + lng[a, steps - 1].astype(F32)
            if steps > 1:
                chain_copy(False, a, steps - 2).wait_recv()
                total = total + sht[a, steps - 2].astype(F32)
            for i in range(div(nx, 2)):
                g2s[a * div(nx, 2) + i] = total[:, i * cb:(i + 1) * cb].astype(BF)

        @pl.loop(0, nx)
        def _(j):
            @pl.when(jnp.logical_not((j == x) & untwisted))
            def _():
                ga_copy(j, x).start()

        @pl.when(untwisted)
        def _():
            ga[x] = g2s[x]

    def along_z():
        @pl.loop(0, nx)
        def _(j):
            @pl.when(jnp.logical_not((j == x) & untwisted))
            def _():
                ga_copy(j, j).wait_recv()

            @pl.when(j != h)
            def _():
                gb_copy(j, h).start()

        gb[h] = ga[h]

    work = [functools.partial(chain_step, t) for t in range(1, steps)] + [chain_end, along_z]
    rows = [functools.partial(far_out, k) for k in range(nq)]
    rows += [functools.partial(far_back, k) for k in range(nq)]
    rows += [functools.partial(near_rows, k) for k in range(nq)]
    for step in work[:2] + [weights_arrived] + rows[:3] + work[2:3] + rows[3:4] + work[3:4] + rows[4:5] + work[4:] + rows[5:]:
        step()
    ret_rcv[me] = ret_snd[me]

    for k in range(1, nh):
        w1_copy(k, h).wait_send()

    @pl.when(jnp.logical_not((x == h) & untwisted))
    def _():
        wo_copy(x).wait_send()

    @pl.loop(0, nsame)
    def _(i):
        p, far = of_core(i, c), of_core(i, 1 - c)
        d_forward(i, p).wait_send()
        d_scaled(far, me, sibling).wait_send()

        @pl.when(p != me)
        def _():
            d_whole(p, me, sibling).wait_send()

    @pl.loop(0, nx * nl)
    def _(i):
        @pl.when(w2_sent(div(i, nl), w2_delta(div(i, nl), rem(i, nl))))
        def _():
            w2_copy(0, 0, 0, 0, i, 0).wait_send()

    for a in range(2):
        for t in range(steps):
            chain_copy(True, a, t).wait_send()
            if t < steps - 1:
                chain_copy(False, a, t).wait_send()

    @pl.loop(0, nsame)
    def _(k):
        p = of_core(rem(me_same - k + nsame, nsame), 1 - c)
        r_out(p, p, sibling).wait_recv()

    @pl.loop(1, nsame)
    def _(k):
        p = of_core(rem(me_same - k + nsame, nsame), c)
        r_whole(p, p, sibling).wait_recv()

    for q in range(ny):
        rows = ret_rcv[q * ne:(q + 1) * ne, :, 0:dc].reshape(ne * cap, dc)
        token_out = gate * dot(placing, rows, ((0,), (0,)))
        for xx in range(nx):
            s0 = (xx * ny + q) * cb
            mixed_ref[:, s0:s0 + cb] = token_out[:, xx * cb:(xx + 1) * cb].astype(BF)
    back = ret_rcv[pl.ds(c * ne, ne), :, dc:dc + fdim].astype(F32)
    for k in range(1, nq):
        back = back + ret_rcv[pl.ds((2 * k + c) * ne, ne), :, dc:dc + fdim].astype(F32)
    back = back.reshape(ne * cap, fdim).astype(BF)
    hg_ref[...] = dot(placing, back, ((0,), (0,))).astype(BF)

    @pl.loop(0, nh)
    def _(hs):
        @pl.when(hs != h)
        def _():
            gb_copy(0, hs).wait_recv()

    total = gb[0].astype(F32)
    for hs in range(1, nh):
        total = total + gb[hs].astype(F32)
    cg_ref[0] = total * scale

    @pl.loop(0, nsame)
    def _(i):
        p, far = of_core(i, c), of_core(i, 1 - c)
        r_out(far, me, sibling).wait_send()

        @pl.when(p != me)
        def _():
            r_whole(p, me, sibling).wait_send()

    @pl.loop(0, nq)
    def _(k):
        x_copy(k).wait_send()

    @pl.loop(0, nx)
    def _(j):
        @pl.when(jnp.logical_not((j == x) & untwisted))
        def _():
            ga_copy(j, x).wait_send()

        @pl.when(j != h)
        def _():
            gb_copy(j, h).wait_send()


def body(nl, nh, nx, ny, hidden_in, expert_ids, gate_prob, out_grad, codes, scales):
    tok, fdim = hidden_in.shape
    ddim = out_grad.shape[1]
    cb = codes.shape[2]
    dc = nx * cb
    ne = 2 * nx
    npl = ny * ne
    cap = 3 * tok // (2 * ne)
    fb = fdim // nl
    dma = pltpu.SemaphoreType.DMA
    vmem = pl.BlockSpec(memory_space=pltpu.VMEM)
    hbm = pl.BlockSpec(memory_space=pl.ANY)
    return pl.pallas_call(
        functools.partial(kernel, nl, nh, nx, ny),
        out_shape=(
            jax.ShapeDtypeStruct((tok, ddim), BF),
            jax.ShapeDtypeStruct((tok, fdim), BF),
            jax.ShapeDtypeStruct((1, fb, cb), F32),
        ),
        in_specs=[vmem, vmem, hbm, hbm, hbm, vmem],
        out_specs=(vmem,) * 3,
        scratch_shapes=[
            pltpu.VMEM((tok, fdim), BF),
            pltpu.VMEM((tok, ddim), BF),
            pltpu.VMEM((fdim, cb), BF),
            pltpu.VMEM((npl, cap, fdim + dc), BF),
            pltpu.VMEM((npl, cap, fdim + dc), BF),
            pltpu.VMEM((npl, cap, fdim + dc), BF),
            pltpu.VMEM((npl, cap, fdim + dc), BF),
            pltpu.VMEM((ny // 2, ne, cap, fdim), BF),
            pltpu.VMEM((ny // 2, ne, cap, fdim), BF),
            pltpu.VMEM((fdim, cb), BF),
            pltpu.VMEM((nh, fb, cb), BF),
            pltpu.VMEM((fdim, dc), BF),
            pltpu.VMEM((2, nl, fb, dc // 2), BF),
            pltpu.VMEM((2, nl // 2, fb, dc // 2), BF),
            pltpu.VMEM((2, nl // 2, fb, dc // 2), BF),
            pltpu.VMEM((nx, fb, cb), BF),
            pltpu.VMEM((nx, fb, cb), BF),
            pltpu.VMEM((nh, fb, cb), BF),
            dma((3,)), dma((npl,)), dma((npl,)), dma((npl // 2,)), dma((npl // 2,)),
            dma((npl,)), dma((npl,)), dma((ny // 2,)), dma((ny // 2,)),
            dma((nh,)), dma((nh,)), dma(()), dma((nx,)), dma((nx * nl,)), dma((nx * nl,)),
            dma((2, nl // 2)), dma((2, nl // 2)), dma((2, nl // 2)), dma((2, nl // 2)), dma((nx,)), dma((nx,)), dma((nx,)), dma((nh,)),
        ],
        compiler_params=pltpu.CompilerParams(
            collective_id=0, has_side_effects=True, vmem_limit_bytes=60 * 2**20
        ),
        cost_estimate=pl.CostEstimate(
            flops=6 * npl * cap * fdim * dc, bytes_accessed=4 * tok * ddim, transcendentals=0
        ),
    )(
        expert_ids.reshape(1, tok), gate_prob.reshape(1, tok), hidden_in, out_grad, codes, scales
    )


def solution(mesh):
    nl, nh = mesh.shape["rep"], mesh.shape["node"] // 2
    nx = nh
    ny = mesh.shape["shard"] // nx
    return jax.shard_map(
        functools.partial(body, nl, nh, nx, ny),
        mesh=mesh,
        in_specs=(
            P(("rep", "node", "shard"), None),
            P(("rep", "node", "shard"), None),
            P(("rep", "node", "shard")),
            P(("rep", "node", "shard"), None),
            P("node", None, "shard"),
            P("node", None),
        ),
        out_specs=(
            P(("rep", "node", "shard"), None),
            P(("rep", "node", "shard"), None),
            P("node", "rep", "shard"),
        ),
        check_vma=False,
    )
```

```python
import functools

import jax
import jax.numpy as jnp
from jax import lax
from jax.experimental import pallas as pl
from jax.experimental.pallas import tpu as pltpu
from jax.sharding import PartitionSpec as P

MESH = pl.DeviceIdType.MESH
BF = jnp.bfloat16
F32 = jnp.float32


def dot(a, b, dims):
    return lax.dot_general(a, b, (dims, ((), ())), preferred_element_type=F32)


def div(a, b):
    return a // b if isinstance(a, int) else lax.div(a, b)


def rem(a, b):
    return a % b if isinstance(a, int) else lax.rem(a, b)


def kernel(
    nl, nh, nx, ny,
    ids_ref, gate_ref, hid_hbm, og_hbm, codes_hbm, scales_ref,
    mixed_ref, hg_ref, cg_ref,
    hid_ref, og_ref, codes_ref,
    snd, rcv, ret_snd, ret_rcv, xb_snd, xb_rcv, wown, w1, wf, tsnd, lng, sht, g2s, ga, gb,
    in_s, d_ss, d_rs, f_ss, f_rs, r_ss, r_rs, rb_ss, rb_rs, x_ss, x_rs,
    w1_ss, w1_rs, wo_ss, wo_rs, w2_ss, w2_rs, lg_ss, lg_rs, sh_ss, sh_rs, ga_ss, ga_rs, gb_ss, gb_rs,
):
    ne = 2 * nx
    npl = ny * ne
    nsame = div(npl, 2)
    nq = div(ny, 2)
    nz = nh * nl
    tok, fdim = hid_ref.shape
    cap = snd.shape[1]
    cb = codes_ref.shape[1]
    fb = div(fdim, nl)
    dc = nx * cb
    hc = div(dc, 2)
    steps = div(nl, 2)

    zl = lax.axis_index("rep")
    node = lax.axis_index("node")
    shard = lax.axis_index("shard")
    h, c = div(node, 2), rem(node, 2)
    x, y = div(shard, ny), rem(shard, ny)
    z = h * nl + zl
    quarter = div(y, 2) * 2 + c
    me = quarter * ne + x * 2 + rem(y, 2)
    me_same = div(quarter, 2) * ne + x * 2 + rem(y, 2)
    ty, tc = div(y, 2) * 2 + c, rem(y, 2)
    untwisted = rem(y, 2) == c

    def dev(xx, yy, zz, cc):
        return (rem(zz, nl), div(zz, nl) * 2 + cc, xx * ny + yy)

    sibling = dev(x, y, z, 1 - c)

    def plane(p):
        q, e = div(p, ne), rem(p, ne)
        return dev(div(e, 2), div(q, 2) * 2 + rem(e, 2), z, rem(q, 2))

    def of_core(i, core):
        return (div(i, ne) * 2 + core) * ne + rem(i, ne)

    def w2_delta(hh, dk):
        return dk - (div(nl, 2) - 1) - rem(hh, 2)

    def w1_turn(k):
        return (2 * c - 1) if 2 * k == nh else 0

    way = 1 - 2 * c

    frow = pl.multiple_of(zl * fb, fb)
    loads = (
        pltpu.make_async_copy(codes_hbm.at[0], codes_ref, in_s.at[0]),
        pltpu.make_async_copy(hid_hbm, hid_ref, in_s.at[1]),
        pltpu.make_async_copy(og_hbm, og_ref, in_s.at[2]),
    )
    for load in loads:
        load.start()

    barrier = pltpu.get_barrier_semaphore()

    def signal(target):
        pl.semaphore_signal(barrier, inc=1, device_id=target, device_id_type=MESH)

    def w2_self(hh, delta):
        return (hh == x) & untwisted & (delta == 0)

    @pl.loop(1, npl)
    def _(k):
        signal(plane(rem(me + k, npl)))

    for k in range(1, nh):
        signal(dev(x, y, rem(h - k + nh, nh) * nl + rem(zl - w1_turn(k) + nl, nl), c))
        signal(dev(x, y, rem(h + k, nh) * nl + zl, c))

    @pl.loop(0, nx * nl)
    def _(i):
        xs, delta = div(i, nl), w2_delta(x, rem(i, nl))

        @pl.when(jnp.logical_not(w2_self(xs, delta)))
        def _():
            signal(dev(xs, ty, rem(z - delta + nz, nz), tc))

    signal(dev(x, y, rem(z + 1, nz), c))
    signal(dev(x, y, rem(z - 1 + nz, nz), c))

    ids = ids_ref[...]
    erows = lax.broadcasted_iota(jnp.int32, (16, tok), 0)
    onehot = (erows == ids).astype(F32)
    ti = lax.broadcasted_iota(jnp.int32, (tok, tok), 0)
    tj = lax.broadcasted_iota(jnp.int32, (tok, tok), 1)
    upto = (ti <= tj).astype(BF)
    count = dot(onehot.astype(BF), upto, ((1,), (0,)))
    rank = jnp.sum(count * onehot, axis=0, keepdims=True) - 1.0
    target = ids * cap + rank.astype(jnp.int32)
    slots = lax.broadcasted_iota(jnp.int32, (ne * cap, tok), 0)
    placing = (slots == target).astype(BF)
    gate = jnp.sum(jnp.where(ti == tj, gate_ref[...], 0.0), axis=1, keepdims=True)

    fi = lax.broadcasted_iota(jnp.int32, (fb, fdim), 0) + zl * fb
    fj = lax.broadcasted_iota(jnp.int32, (fb, fdim), 1)
    scale = jnp.sum(jnp.where(fi == fj, scales_ref[...], 0.0), axis=1, keepdims=True)
    loads[0].wait()
    wide = min(128, fdim)
    eye_r = lax.broadcasted_iota(jnp.int32, (wide, wide), 0)
    eye_c = lax.broadcasted_iota(jnp.int32, (wide, wide), 1)
    for f0 in range(0, fdim, wide):
        col = jnp.where(eye_r == eye_c, scales_ref[:, f0:f0 + wide], 0.0)
        col = jnp.sum(col, axis=1, keepdims=True)
        wown[f0:f0 + wide] = (codes_ref[f0:f0 + wide].astype(F32) * col).astype(BF)
    w1[h] = wown[pl.ds(frow, fb)]

    loads[1].wait()
    hid_rows = dot(placing, hid_ref[...], ((1,), (0,))).astype(BF).reshape(ne, cap, fdim)
    for k in range(nq):
        snd[pl.ds((2 * k + c) * ne, ne), :, 0:fdim] = hid_rows
    loads[2].wait()
    for q in range(ny):
        for xx in range(nx):
            s0 = (xx * ny + q) * cb
            cols = (gate * og_ref[:, s0:s0 + cb].astype(F32)).astype(BF)
            rows = dot(placing, cols, ((1,), (0,))).astype(BF).reshape(ne, cap, cb)
            snd[q * ne:(q + 1) * ne, :, fdim + xx * cb:fdim + (xx + 1) * cb] = rows
    rcv[me] = snd[me]

    pl.semaphore_wait(
        barrier,
        (npl - 1) + 2 * (nh - 1) + (nx * nl - jnp.where(untwisted, 1, 0)) + 2,
    )

    def w1_copy(k, slot):
        row = rem(zl + w1_turn(k) + nl, nl)
        return pltpu.make_async_remote_copy(
            src_ref=wown.at[pl.ds(pl.multiple_of(row * fb, fb), fb)], dst_ref=w1.at[slot],
            send_sem=w1_ss.at[k], recv_sem=w1_rs.at[slot],
            device_id=dev(x, y, rem(h + k, nh) * nl + row, c), device_id_type=MESH,
        )

    def wo_copy(xcol):
        return pltpu.make_async_remote_copy(
            src_ref=wown, dst_ref=wf.at[:, pl.ds(pl.multiple_of(xcol * cb, cb), cb)],
            send_sem=wo_ss, recv_sem=wo_rs.at[xcol],
            device_id=dev(h, ty, z, tc), device_id_type=MESH,
        )

    near_first = sorted(range(1, nh), key=lambda k: -abs(2 * k - nh))
    for k in reversed(near_first):
        w1_copy(k, h).start()

    def d_whole(p, slot, target=None):
        return pltpu.make_async_remote_copy(
            src_ref=snd.at[p], dst_ref=rcv.at[slot],
            send_sem=d_ss.at[p], recv_sem=d_rs.at[slot],
            device_id=target or plane(p), device_id_type=MESH,
        )

    def d_scaled(p, slot, target=None):
        return pltpu.make_async_remote_copy(
            src_ref=snd.at[p, :, pl.ds(fdim, dc)], dst_ref=rcv.at[slot, :, pl.ds(fdim, dc)],
            send_sem=d_ss.at[p], recv_sem=d_rs.at[slot],
            device_id=target or plane(p), device_id_type=MESH,
        )

    def d_forward(i, slot):
        return pltpu.make_async_remote_copy(
            src_ref=rcv.at[slot, :, pl.ds(0, fdim)], dst_ref=rcv.at[slot, :, pl.ds(0, fdim)],
            send_sem=f_ss.at[i], recv_sem=f_rs.at[i],
            device_id=sibling, device_id_type=MESH,
        )

    d_forward(me_same, me).start()

    @pl.loop(1, nsame)
    def _(k):
        d_whole(of_core(rem(me_same + k, nsame), c), me).start()

    @pl.loop(0, nsame)
    def _(k):
        d_scaled(of_core(rem(me_same + k, nsame), 1 - c), me).start()

    @pl.when(jnp.logical_not((x == h) & untwisted))
    def _():
        wo_copy(x).start()

    @pl.when((x == h) & untwisted)
    def _():
        wf[:, pl.ds(pl.multiple_of(x * cb, cb), cb)] = wown[...]

    def w2_copy(hh, delta, fblk, xcol, sem_i, sem_r):
        return pltpu.make_async_remote_copy(
            src_ref=w1.at[hh],
            dst_ref=wf.at[
                pl.ds(pl.multiple_of(fblk * fb, fb), fb), pl.ds(pl.multiple_of(xcol * cb, cb), cb)
            ],
            send_sem=w2_ss.at[sem_i], recv_sem=w2_rs.at[sem_r],
            device_id=dev(hh, ty, rem(z + delta + nz, nz), tc), device_id_type=MESH,
        )

    def w2_sent(hh, delta):
        segment = div(rem(z + delta + nz, nz), nl)
        return (segment != hh) & jnp.logical_not(w2_self(hh, delta))

    def w2_send(hh):
        @pl.loop(0, nl)
        def _(dk):
            delta = w2_delta(hh, dk)

            @pl.when(w2_sent(hh, delta))
            def _():
                w2_copy(hh, delta, zl, x, hh * nl + dk, x * nl + zl).start()

    w2_send(h)
    for k in near_first:
        other = rem(h + nh - k, nh)
        w1_copy(k, other).wait_recv()
        w2_send(other)

    @pl.when((x != h) & untwisted)
    def _():
        wf[pl.ds(frow, fb), pl.ds(pl.multiple_of(x * cb, cb), cb)] = w1[x]

    @pl.loop(1, nsame)
    def _(k):
        i = rem(me_same - k + nsame, nsame)
        p = of_core(i, c)
        d_whole(p, p, sibling).wait_recv()
        d_forward(i, p).start()

    @pl.loop(0, nsame)
    def _(k):
        p = of_core(rem(me_same - k + nsame, nsame), 1 - c)
        d_scaled(p, p, sibling).wait_recv()

    @pl.loop(0, nsame)
    def _(i):
        d_forward(i, of_core(i, 1 - c)).wait_recv()

    def chain_copy(long, a, t):
        toward = way if long else -way
        d = (steps if long else steps - 1) - t
        slot, ss, rs = (lng, lg_ss, lg_rs) if long else (sht, sh_ss, sh_rs)
        return pltpu.make_async_remote_copy(
            src_ref=tsnd.at[a, rem(zl + toward * d + nl, nl)], dst_ref=slot.at[a, t],
            send_sem=ss.at[a, t], recv_sem=rs.at[a, t],
            device_id=dev(x, y, rem(z + toward + nz, nz), c), device_id_type=MESH,
        )

    def chain_step(t):
        for a in range(2):
            for long in (True, False):
                length = steps if long else steps - 1
                if t < length:
                    toward = way if long else -way
                    piece = rem(zl + toward * (length - t) + nl, nl)
                    slot = lng if long else sht
                    chain_copy(long, a, t - 1).wait_recv()
                    both = tsnd[a, piece].astype(F32) + slot[a, t - 1].astype(F32)
                    tsnd[a, piece] = both.astype(BF)
                    chain_copy(long, a, t).start()

    fchunk = div(fdim, 2)
    for a in range(2):
        lanes = slice(fdim + a * hc, fdim + (a + 1) * hc)
        sc_a = rcv[:, :, lanes].reshape(npl * cap, hc)
        for k in range(2):
            hid_c = rcv[:, :, k * fchunk:(k + 1) * fchunk].reshape(npl * cap, fchunk)
            t = dot(hid_c, sc_a, ((0,), (0,))).astype(BF)
            tsnd[a, k * div(nl, 2):(k + 1) * div(nl, 2)] = t.reshape(div(nl, 2), fb, hc)
        chain_copy(True, a, 0).start()
        if steps > 1:
            chain_copy(False, a, 0).start()

    def weights_arrived():
        @pl.when(x == h)
        def _():
            @pl.loop(0, nx)
            def _(i):
                @pl.when(jnp.logical_not(untwisted & (i == x)))
                def _():
                    wo_copy(i).wait_recv()

        @pl.when(x != h)
        def _():
            @pl.loop(0, nx * nl)
            def _(i):
                @pl.when(jnp.logical_not(untwisted & (i == x * nl + zl)))
                def _():
                    w2_copy(0, 0, rem(i, nl), div(i, nl), i, i).wait_recv()

    def x_copy(k):
        return pltpu.make_async_remote_copy(
            src_ref=xb_snd.at[k], dst_ref=xb_rcv.at[k],
            send_sem=x_ss.at[k], recv_sem=x_rs.at[k],
            device_id=sibling, device_id_type=MESH,
        )

    def r_back(p, slot, target=None):
        return pltpu.make_async_remote_copy(
            src_ref=ret_snd.at[p, :, pl.ds(dc, fdim)], dst_ref=ret_rcv.at[slot, :, pl.ds(dc, fdim)],
            send_sem=rb_ss.at[p], recv_sem=rb_rs.at[slot],
            device_id=target or plane(p), device_id_type=MESH,
        )

    def r_out(p, slot, target=None):
        return pltpu.make_async_remote_copy(
            src_ref=ret_snd.at[p, :, pl.ds(0, dc)], dst_ref=ret_rcv.at[slot, :, pl.ds(0, dc)],
            send_sem=r_ss.at[p], recv_sem=r_rs.at[slot],
            device_id=target or plane(p), device_id_type=MESH,
        )

    def far_out(k):
        p0 = (2 * k + 1 - c) * ne
        hid_c = rcv[pl.ds(p0, ne), :, 0:fdim].reshape(ne * cap, fdim)
        o = dot(hid_c, wf[...], ((1,), (0,))).astype(BF)
        ret_snd[pl.ds(p0, ne), :, 0:dc] = o.reshape(ne, cap, dc)

        @pl.loop(0, ne)
        def _(i):
            r_out(p0 + rem(me + i, ne), me).start()

    def far_back(k):
        p0 = (2 * k + 1 - c) * ne
        sc_c = rcv[pl.ds(p0, ne), :, fdim:fdim + dc].reshape(ne * cap, dc)
        b = dot(sc_c, wf[...], ((1,), (1,))).astype(BF)
        xb_snd[k] = b.reshape(ne, cap, fdim)
        x_copy(k).start()

    def near_out(k):
        p0 = (2 * k + c) * ne
        hid_c = rcv[pl.ds(p0, ne), :, 0:fdim].reshape(ne * cap, fdim)
        o = dot(hid_c, wf[...], ((1,), (0,))).astype(BF)
        ret_snd[pl.ds(p0, ne), :, 0:dc] = o.reshape(ne, cap, dc)

        @pl.loop(0, ne)
        def _(i):
            p = p0 + rem(me + i, ne)

            @pl.when(p != me)
            def _():
                r_out(p, me).start()

    def near_back(k):
        p0 = (2 * k + c) * ne
        sc_c = rcv[pl.ds(p0, ne), :, fdim:fdim + dc].reshape(ne * cap, dc)
        b = dot(sc_c, wf[...], ((1,), (1,)))
        x_copy(k).wait_recv()
        b = b.reshape(ne, cap, fdim) + xb_rcv[k].astype(F32)
        ret_snd[pl.ds(p0, ne), :, dc:dc + fdim] = b.astype(BF)

        @pl.loop(0, ne)
        def _(i):
            p = p0 + rem(me + i, ne)

            @pl.when(p != me)
            def _():
                r_back(p, me).start()

    def ga_copy(j, slot):
        return pltpu.make_async_remote_copy(
            src_ref=g2s.at[j], dst_ref=ga.at[slot],
            send_sem=ga_ss.at[j], recv_sem=ga_rs.at[slot],
            device_id=dev(j, ty, z, tc), device_id_type=MESH,
        )

    def gb_copy(j, slot):
        return pltpu.make_async_remote_copy(
            src_ref=ga.at[j], dst_ref=gb.at[slot],
            send_sem=gb_ss.at[j], recv_sem=gb_rs.at[slot],
            device_id=dev(x, y, j * nl + zl, c), device_id_type=MESH,
        )

    def chain_end():
        for a in range(2):
            total = tsnd[a, zl].astype(F32)
            chain_copy(True, a, steps - 1).wait_recv()
            total = total + lng[a, steps - 1].astype(F32)
            if steps > 1:
                chain_copy(False, a, steps - 2).wait_recv()
                total = total + sht[a, steps - 2].astype(F32)
            for i in range(div(nx, 2)):
                g2s[a * div(nx, 2) + i] = total[:, i * cb:(i + 1) * cb].astype(BF)

        @pl.loop(0, nx)
        def _(j):
            @pl.when(jnp.logical_not((j == x) & untwisted))
            def _():
                ga_copy(j, x).start()

        @pl.when(untwisted)
        def _():
            ga[x] = g2s[x]

    def along_z():
        @pl.loop(0, nx)
        def _(j):
            @pl.when(jnp.logical_not((j == x) & untwisted))
            def _():
                ga_copy(j, j).wait_recv()

            @pl.when(j != h)
            def _():
                gb_copy(j, h).start()

        gb[h] = ga[h]

    work = [functools.partial(chain_step, t) for t in range(1, steps)] + [chain_end, along_z]
    rows = [functools.partial(far_out, k) for k in range(nq)]
    rows += [functools.partial(far_back, k) for k in range(nq)]
    rows += [functools.partial(near_out, k) for k in range(nq)]
    rows += [functools.partial(near_back, k) for k in range(nq)]
    order = work[:2] + [weights_arrived] + rows[:3] + work[2:3] + rows[3:4]
    for step in order + work[3:4] + rows[4:6] + work[4:] + rows[6:]:
        step()
    ret_rcv[me] = ret_snd[me]

    for k in range(1, nh):
        w1_copy(k, h).wait_send()

    @pl.when(jnp.logical_not((x == h) & untwisted))
    def _():
        wo_copy(x).wait_send()

    @pl.loop(0, nsame)
    def _(i):
        p, far = of_core(i, c), of_core(i, 1 - c)
        d_forward(i, p).wait_send()
        d_scaled(far, me, sibling).wait_send()

        @pl.when(p != me)
        def _():
            d_whole(p, me, sibling).wait_send()

    @pl.loop(0, nx * nl)
    def _(i):
        @pl.when(w2_sent(div(i, nl), w2_delta(div(i, nl), rem(i, nl))))
        def _():
            w2_copy(0, 0, 0, 0, i, 0).wait_send()

    for a in range(2):
        for t in range(steps):
            chain_copy(True, a, t).wait_send()
            if t < steps - 1:
                chain_copy(False, a, t).wait_send()

    @pl.loop(0, nsame)
    def _(k):
        p = of_core(rem(me_same - k + nsame, nsame), 1 - c)
        r_out(p, p, sibling).wait_recv()

    @pl.loop(1, nsame)
    def _(k):
        p = of_core(rem(me_same - k + nsame, nsame), c)
        r_out(p, p, sibling).wait_recv()
        r_back(p, p, sibling).wait_recv()

    for q in range(ny):
        rows = ret_rcv[q * ne:(q + 1) * ne, :, 0:dc].reshape(ne * cap, dc)
        token_out = gate * dot(placing, rows, ((0,), (0,)))
        for xx in range(nx):
            s0 = (xx * ny + q) * cb
            mixed_ref[:, s0:s0 + cb] = token_out[:, xx * cb:(xx + 1) * cb].astype(BF)
    back = ret_rcv[pl.ds(c * ne, ne), :, dc:dc + fdim].astype(F32)
    for k in range(1, nq):
        back = back + ret_rcv[pl.ds((2 * k + c) * ne, ne), :, dc:dc + fdim].astype(F32)
    back = back.reshape(ne * cap, fdim).astype(BF)
    hg_ref[...] = dot(placing, back, ((0,), (0,))).astype(BF)

    @pl.loop(0, nh)
    def _(hs):
        @pl.when(hs != h)
        def _():
            gb_copy(0, hs).wait_recv()

    total = gb[0].astype(F32)
    for hs in range(1, nh):
        total = total + gb[hs].astype(F32)
    cg_ref[0] = total * scale

    @pl.loop(0, nsame)
    def _(i):
        p, far = of_core(i, c), of_core(i, 1 - c)
        r_out(far, me, sibling).wait_send()

        @pl.when(p != me)
        def _():
            r_out(p, me, sibling).wait_send()
            r_back(p, me, sibling).wait_send()

    @pl.loop(0, nq)
    def _(k):
        x_copy(k).wait_send()

    @pl.loop(0, nx)
    def _(j):
        @pl.when(jnp.logical_not((j == x) & untwisted))
        def _():
            ga_copy(j, x).wait_send()

        @pl.when(j != h)
        def _():
            gb_copy(j, h).wait_send()


def body(nl, nh, nx, ny, hidden_in, expert_ids, gate_prob, out_grad, codes, scales):
    tok, fdim = hidden_in.shape
    ddim = out_grad.shape[1]
    cb = codes.shape[2]
    dc = nx * cb
    ne = 2 * nx
    npl = ny * ne
    cap = 3 * tok // (2 * ne)
    fb = fdim // nl
    dma = pltpu.SemaphoreType.DMA
    vmem = pl.BlockSpec(memory_space=pltpu.VMEM)
    hbm = pl.BlockSpec(memory_space=pl.ANY)
    return pl.pallas_call(
        functools.partial(kernel, nl, nh, nx, ny),
        out_shape=(
            jax.ShapeDtypeStruct((tok, ddim), BF),
            jax.ShapeDtypeStruct((tok, fdim), BF),
            jax.ShapeDtypeStruct((1, fb, cb), F32),
        ),
        in_specs=[vmem, vmem, hbm, hbm, hbm, vmem],
        out_specs=(vmem,) * 3,
        scratch_shapes=[
            pltpu.VMEM((tok, fdim), BF),
            pltpu.VMEM((tok, ddim), BF),
            pltpu.VMEM((fdim, cb), BF),
            pltpu.VMEM((npl, cap, fdim + dc), BF),
            pltpu.VMEM((npl, cap, fdim + dc), BF),
            pltpu.VMEM((npl, cap, fdim + dc), BF),
            pltpu.VMEM((npl, cap, fdim + dc), BF),
            pltpu.VMEM((ny // 2, ne, cap, fdim), BF),
            pltpu.VMEM((ny // 2, ne, cap, fdim), BF),
            pltpu.VMEM((fdim, cb), BF),
            pltpu.VMEM((nh, fb, cb), BF),
            pltpu.VMEM((fdim, dc), BF),
            pltpu.VMEM((2, nl, fb, dc // 2), BF),
            pltpu.VMEM((2, nl // 2, fb, dc // 2), BF),
            pltpu.VMEM((2, nl // 2, fb, dc // 2), BF),
            pltpu.VMEM((nx, fb, cb), BF),
            pltpu.VMEM((nx, fb, cb), BF),
            pltpu.VMEM((nh, fb, cb), BF),
            dma((3,)), dma((npl,)), dma((npl,)), dma((npl // 2,)), dma((npl // 2,)),
            dma((npl,)), dma((npl,)), dma((npl,)), dma((npl,)), dma((ny // 2,)), dma((ny // 2,)),
            dma((nh,)), dma((nh,)), dma(()), dma((nx,)), dma((nx * nl,)), dma((nx * nl,)),
            dma((2, nl // 2)), dma((2, nl // 2)), dma((2, nl // 2)), dma((2, nl // 2)), dma((nx,)), dma((nx,)), dma((nx,)), dma((nh,)),
        ],
        compiler_params=pltpu.CompilerParams(
            collective_id=0, has_side_effects=True, vmem_limit_bytes=60 * 2**20
        ),
        cost_estimate=pl.CostEstimate(
            flops=6 * npl * cap * fdim * dc, bytes_accessed=4 * tok * ddim, transcendentals=0
        ),
    )(
        expert_ids.reshape(1, tok), gate_prob.reshape(1, tok), hidden_in, out_grad, codes, scales
    )


def solution(mesh):
    nl, nh = mesh.shape["rep"], mesh.shape["node"] // 2
    nx = nh
    ny = mesh.shape["shard"] // nx
    return jax.shard_map(
        functools.partial(body, nl, nh, nx, ny),
        mesh=mesh,
        in_specs=(
            P(("rep", "node", "shard"), None),
            P(("rep", "node", "shard"), None),
            P(("rep", "node", "shard")),
            P(("rep", "node", "shard"), None),
            P("node", None, "shard"),
            P("node", None),
        ),
        out_specs=(
            P(("rep", "node", "shard"), None),
            P(("rep", "node", "shard"), None),
            P("node", "rep", "shard"),
        ),
        check_vma=False,
    )
```
